32 devices in a mesh: row: 8 (over y, x, core), col: 4 (over z).
Axes of the slice: x: 2, y: 2, z: 4, core: 2. Of those that a mesh axis runs over, the one named last changes fastest.
Arguments:
- node_features: bfloat16 [32768, 256], P(('row', 'col')), may hold values from -6 to 6
- tile_cols: int32 [512, 8], P(('row', 'col')), may hold values from 0 to 511, as said below
- tile_weights: int32 [512, 64, 512], P(('row', 'col')), may hold values from 0 to 7
- w_self: bfloat16 [256, 1024], replicated, may hold values from -0.375 to 0.375
- w_neigh: bfloat16 [256, 1024], replicated, may hold values from -0.375 to 0.375
- bias_hidden: float32 [1024], replicated, may hold values from -3 to 3
- w_out: bfloat16 [1024, 256], replicated, may hold values from -0.1875 to 0.1875
- bias_out: float32 [256], replicated, may hold values from -3 to 3
- cotangent: bfloat16 [32768, 256], P(('row', 'col')), may hold values from -6 to 6
Outputs:
- embed: bfloat16 [32768, 256], P(('row', 'col'))
- grad_features: bfloat16 [32768, 256], P(('row', 'col'))
- grad_w_self: float32 [256, 1024], replicated
- grad_w_neigh: float32 [256, 1024], replicated
- grad_bias_hidden: float32 [1024], replicated
- grad_w_out: float32 [1024, 256], replicated
- grad_bias_out: float32 [256], replicated
The draws below stay inside these ranges and needn't reach their ends.
Inputs may be any that keep to these rules, and one draw needn't show every extreme that they name: `tile_cols`: the first tile of block row b is its diagonal block b. The second lies exactly 16 block rows before or after b (the side drawn for each row), clipped to the graph. Every tile's block column differs from its block row by at most 16.
All inputs are finite; a program needn't handle non-finite values.
Results may differ from the reference program's by a relative error of at most 0.0071.
Values may be sent and summed in bfloat16 or wider, within the bound.
No kernel may reach another device: no remote copies, remote signals or barrier semaphores. Data moves between devices by JAX's collectives and lax.ppermute only.
A program may use at most 128 MiB of HBM per device.

```python
import math
import jax
import jax.numpy as jnp
from jax import lax

F = 256
HID = 1024
TILE = 64
TPB = 8
CH = 1024
CB = 16
NB = 512
NODES = 32768


def draw_tile_cols(key, part):
    first_key, second_key = jax.random.split(key, 2)
    block_index = jnp.arange(NB, dtype=jnp.int32)[:, None]
    slot_index = jnp.arange(TPB, dtype=jnp.int32)[None, :]
    offsets = jax.random.randint(first_key, (NB, TPB), -CB, CB + 1, dtype=jnp.int32)
    sides = jax.random.randint(second_key, (NB, 1), 0, 2, dtype=jnp.int32) * 2 - 1
    offsets = jnp.where(slot_index == 0, 0, jnp.where(slot_index == 1, sides * CB, offsets))
    return jnp.clip(block_index + offsets, 0, NB - 1).astype(jnp.int32)


def plant(array, own_key, low, largest):
    shape = array.shape
    spot = [jax.random.randint(jax.random.fold_in(own_key, axis), (), 0, shape[axis]) for axis in range(len(shape))]
    array = array.at[tuple(spot)].set(low)
    longest = shape.index(max(shape))
    spot[longest] = (spot[longest] + 1) % shape[longest]
    return array.at[tuple(spot)].set(largest)


def level_of(own_key, dims, cuts, low, top_value):
    loudness, own = 1.0, jax.random.fold_in(own_key, 6)
    for position, parts in cuts:
        draws = jnp.exp(jax.random.uniform(jax.random.fold_in(own, position), (parts,), jnp.float32, low / len(cuts), top_value / len(cuts)))
        loudness = loudness * jnp.repeat(draws, dims[position] // parts).reshape([-1 if axis == position else 1 for axis in range(len(dims))])
    return loudness


def bell_draw(own_key, dims, scale, bound, cuts=(), kind=jnp.bfloat16):
    array = jax.random.normal(own_key, dims, jnp.float32) * scale
    if len(cuts) > 0:
        array = level_of(own_key, dims, cuts, -0.22, 0.18) * array
    return jnp.clip(array, min=-bound, max=bound).astype(kind)


def setup_inputs(seed: int = 0) -> dict:
    keys = jax.random.split(jax.random.key(seed), 10)
    node_features = bell_draw(keys[0], (NODES, F), 1.0, 6.0, ((0, 32),))
    tile_cols = draw_tile_cols(jax.random.fold_in(keys[9], 71), 0)
    tile_weights = plant(jax.random.randint(keys[2], (NB, TILE, TPB * TILE), 0, 8), jax.random.fold_in(keys[2], 1), 0, 7).astype(jnp.int32)
    w_self = bell_draw(keys[3], (F, HID), F ** -0.5, 0.375)
    w_neigh = bell_draw(keys[4], (F, HID), F ** -0.5, 0.375)
    bias_hidden = bell_draw(keys[5], (HID,), 0.5, 3.0, (), jnp.float32)
    w_out = bell_draw(keys[6], (HID, F), HID ** -0.5, 0.1875)
    bias_out = bell_draw(keys[7], (F,), 0.5, 3.0, (), jnp.float32)
    cotangent = bell_draw(keys[8], (NODES, F), 1.0, 6.0, ((0, 32),))
    return {"node_features": node_features, "tile_cols": tile_cols, "tile_weights": tile_weights, "w_self": w_self, "w_neigh": w_neigh, "bias_hidden": bias_hidden, "w_out": w_out, "bias_out": bias_out, "cotangent": cotangent}


def gelu_tanh(values):
    return jax.nn.gelu(values, approximate=True)

def reference(node_features, tile_cols, tile_weights, w_self, w_neigh, bias_hidden, w_out, bias_out, cotangent):
    tile_scale = 0.25 / math.sqrt(TPB * TILE)
    groups = NB // CB
    all_blocks = node_features.reshape(NB, TILE, F)
    group_inputs = (node_features.reshape(groups, CH, F), tile_cols.reshape(groups, CB, TPB), tile_weights.reshape(groups, CB, TILE, TPB * TILE), cotangent.reshape(groups, CH, F))

    def advance(state_pair, inputs):
        partials, adjoint_sum = state_pair
        features, columns, weights, incoming = inputs
        adjacency = (weights.astype(jnp.float32) * tile_scale).astype(jnp.bfloat16)
        gathered = all_blocks[columns].reshape(CB, TPB * TILE, F)
        aggregate = jnp.einsum('bij,bjf->bif', adjacency.astype(jnp.float32), gathered.astype(jnp.float32))
        aggregate = aggregate.reshape(CH, F).astype(jnp.bfloat16)
        preact = jnp.dot(features, w_self, preferred_element_type=jnp.float32) + jnp.dot(aggregate, w_neigh, preferred_element_type=jnp.float32) + bias_hidden
        activated, pullback = jax.vjp(gelu_tanh, preact)
        hidden = activated.astype(jnp.bfloat16)
        embed_rows = (jnp.dot(hidden, w_out, preferred_element_type=jnp.float32) + bias_out).astype(jnp.bfloat16)
        d_act = jnp.dot(incoming, w_out.T, preferred_element_type=jnp.float32)
        d_hidden = pullback(d_act)[0].astype(jnp.bfloat16)
        partials = (partials[0] + jnp.dot(features.T, d_hidden, preferred_element_type=jnp.float32), partials[1] + jnp.dot(aggregate.T, d_hidden, preferred_element_type=jnp.float32), partials[2] + lax.optimization_barrier(jnp.sum(d_hidden.astype(jnp.float32), axis=0)), partials[3] + jnp.dot(hidden.T, incoming, preferred_element_type=jnp.float32), partials[4] + lax.optimization_barrier(jnp.sum(incoming.astype(jnp.float32), axis=0)))
        d_aggregate = jnp.dot(d_hidden, w_neigh.T, preferred_element_type=jnp.float32).astype(jnp.bfloat16)
        d_self = jnp.dot(d_hidden, w_self.T, preferred_element_type=jnp.float32)
        spread = jnp.einsum('bij,bif->bjf', adjacency.astype(jnp.float32), d_aggregate.reshape(CB, TILE, F).astype(jnp.float32))
        spread = spread.reshape(CB * TPB, TILE, F)
        adjoint_sum = adjoint_sum.at[columns.reshape(-1)].add(spread)
        return ((partials, adjoint_sum), (embed_rows, d_self))
    start_partials = (jnp.zeros((F, HID), jnp.float32), jnp.zeros((F, HID), jnp.float32), jnp.zeros((HID,), jnp.float32), jnp.zeros((HID, F), jnp.float32), jnp.zeros((F,), jnp.float32))
    start_adjoint = jnp.zeros((NB, TILE, F), jnp.float32)
    (partials, adjoint_sum), (embed_rows, d_self) = lax.scan(advance, (start_partials, start_adjoint), group_inputs)
    embed = embed_rows.reshape(NODES, F)
    grad_features = (d_self.reshape(NODES, F) + adjoint_sum.reshape(NODES, F)).astype(jnp.bfloat16)
    grad_scale = 1.0 / math.sqrt(NODES)
    return (embed, grad_features, partials[0] * grad_scale, partials[1] * grad_scale, partials[2] * grad_scale, partials[3] * grad_scale, partials[4] * grad_scale)
```

```python
import functools
import math

import jax
import jax.numpy as jnp
from jax import lax
from jax.experimental import pallas as pl
from jax.experimental.pallas import tpu as pltpu
from jax.sharding import PartitionSpec as P

BF16 = jnp.bfloat16
F32 = jnp.float32
GELU_C = math.sqrt(2.0 / math.pi)
GELU_A = 0.044715
VMEM_LIMIT = 40 * 1024 * 1024
LANES = 128
HALVES = 8
QUARTERS = 4


def vmem():
    return pl.BlockSpec(memory_space=pltpu.VMEM)


def smem():
    return pl.BlockSpec(memory_space=pltpu.SMEM)


def params():
    return pltpu.CompilerParams(vmem_limit_bytes=VMEM_LIMIT)


def dot(a, b):
    return jnp.dot(a, b, preferred_element_type=F32)


def prepare_kernel(tile_scale, tw, x, cot, ws, wn, wo, adj, lhs, cot_t, wo_t, w_back, bias_sum):
    for b in range(tw.shape[0]):
        adj[b] = (tw[b].astype(F32) * tile_scale).astype(BF16)
    width = x.shape[1]
    lhs[...] = x[...].T
    cot_t[...] = cot[...].T
    wo_t[...] = wo[...].T
    w_back[:, :width] = wn[...].T
    w_back[:, width:] = ws[...].T
    bias_sum[...] = jnp.sum(cot[...].astype(F32), axis=0, keepdims=True)


def forward_kernel(
    place, cols, lo, x, hi, adj, x_t, cot, cot_t, ws, wn, bias, wo_t, hid, dh, keep, send, bias_sum,
    window, agg, left
):
    rows, width = x.shape
    hidden = ws.shape[1]
    blocks, tile, _ = adj.shape
    slots = cols.shape[1]
    first, me, z = place[0], place[1], place[2]
    window[:rows] = lo[...]
    window[rows : 2 * rows] = x[...]
    window[2 * rows :] = hi[...]
    for b in range(blocks):
        parts = []
        for s in range(slots):
            at = pl.multiple_of((cols[b, s] - first) * tile, tile)
            parts.append(window[pl.ds(at, tile), :])
        agg[b * tile : (b + 1) * tile, :] = dot(adj[b], jnp.concatenate(parts, axis=0)).astype(BF16)
    left[:width] = x_t[...]
    left[width:] = agg[...].T
    chunk = 2 * LANES
    piece = width // QUARTERS
    core = lax.rem(me, 2)
    pair = me // 2

    def one(c, carry):
        at = pl.ds(pl.multiple_of(c * chunk, chunk), chunk)
        ws_c, wn_c, wo_c, bias_c = ws[:, at], wn[:, at], wo_t[:, at], bias[:, at]
        total = jnp.zeros((1, chunk), F32)
        step = 256
        for r in range(0, rows, step):
            sl = slice(r, r + step)
            v = dot(x[sl], ws_c) + dot(agg[sl], wn_c) + bias_c
            da = dot(cot[sl], wo_c)
            sq = v * v
            t = jnp.tanh(v * (GELU_C + (GELU_C * GELU_A) * sq))
            half = 0.5 + 0.5 * t
            hid[sl, at] = (v * half).astype(BF16)
            slope = half + (0.5 * v) * (1.0 - t * t) * (GELU_C + (3.0 * GELU_C * GELU_A) * sq)
            d = (da * slope).astype(BF16)
            dh[sl, at] = d
            total = total + jnp.sum(d.astype(F32), axis=0, keepdims=True)
        bias_sum[:, at] = total
        g = dot(left[...], dh[:, at])
        g_out = dot(cot_t[...], hid[:, at])
        rel = jnp.bitwise_xor(c, pair)
        for t, value in enumerate((g[:width], g[width:], g_out)):
            mine = jnp.where(core == 0, value[:, :LANES], value[:, LANES:])
            other = jnp.where(core == 0, value[:, LANES:], value[:, :LANES]).astype(BF16)
            for k in range(QUARTERS):
                q = jnp.bitwise_xor(k, z)
                keep[rel, q, t * piece : (t + 1) * piece] = mine[k * piece : (k + 1) * piece]
                send[rel, q, t * piece : (t + 1) * piece] = other[k * piece : (k + 1) * piece]
        return carry

    lax.fori_loop(0, hidden // chunk, one, 0)


def backward_kernel(
    place, cols, adj, hid, dh, wo, bias_out, w_back, embed, own, to_low, to_high, total, d_agg
):
    rows, width = embed.shape
    blocks, tile, _ = adj.shape
    slots = cols.shape[1]
    first = place[0]
    step = 256
    for r in range(0, rows, step):
        sl = slice(r, r + step)
        both = dot(dh[sl], w_back[...])
        d_agg[sl] = both[:, :width].astype(BF16)
        total[rows + r : rows + r + step] = both[:, width:]
    total[:rows] = jnp.zeros((rows, width), F32)
    total[2 * rows :] = jnp.zeros((rows, width), F32)
    for b in range(blocks):
        spread = lax.dot_general(
            adj[b], d_agg[b * tile : (b + 1) * tile], (((0,), (0,)), ((), ())), preferred_element_type=F32
        )
        for s in range(slots):
            at = pl.multiple_of((cols[b, s] - first) * tile, tile)
            total[pl.ds(at, tile), :] += spread[s * tile : (s + 1) * tile]
    to_low[...] = total[:rows].astype(BF16)
    to_high[...] = total[2 * rows :].astype(BF16)
    own[...] = total[rows : 2 * rows]
    for r in range(0, rows, step):
        sl = slice(r, r + step)
        embed[sl] = (dot(hid[sl], wo[...]) + bias_out[...]).astype(BF16)


def unpack_kernel(scale, place, mine, other, g_self, g_neigh, g_out, turned):
    width = g_self.shape[0]
    piece = width // QUARTERS
    me, z = place[1], place[2]
    core = lax.rem(me, 2)
    pair = me // 2
    for j in range(HALVES // 2):
        for half, ref in enumerate((mine, other)):
            p = 2 * jnp.bitwise_xor(j, pair) + jnp.bitwise_xor(core, half)
            at = pl.ds(pl.multiple_of(p * LANES, LANES), LANES)
            for k in range(QUARTERS):
                to = pl.ds(pl.multiple_of(jnp.bitwise_xor(k, z) * piece, piece), piece)
                g_self[to, at] = ref[j, k, :piece].astype(F32) * scale
                g_neigh[to, at] = ref[j, k, piece : 2 * piece].astype(F32) * scale
                turned[to, :] = ref[j, k, 2 * piece :].astype(F32) * scale
            g_out[at, :] = turned[...].T


def swap(value, axis, bit):
    return lax.ppermute(value, axis, [(i, i ^ bit) for i in range(lax.axis_size(axis))])


def split(value):
    high = lax.reduce_precision(value, 8, 7)
    return high, lax.reduce_precision(value - high, 8, 7)


def packed(high, low):
    return jnp.concatenate([high.reshape(-1, LANES), low.reshape(-1, LANES)]).astype(BF16)


def swap_with_bias(value, bias, axis, bit):
    high, low = split(bias)
    extra = packed(high, low)
    count = extra.shape[0]
    message = jnp.concatenate([value.reshape(-1, LANES), extra])
    got = swap(message, axis, bit)
    back = got[-count:].astype(F32).reshape((2,) + bias.shape)
    theirs = got[:-count].reshape(value.shape)
    return theirs, (high + low) + (back[0] + back[1])


def all_reduce(keep, send, bias):
    got, bias = swap_with_bias(send, bias, "row", 1)
    acc = keep + got.astype(F32)
    a, b = acc[:, :2], acc[:, 2:]
    got_a, bias = swap_with_bias(a[1::2].astype(BF16), bias, "row", 2)
    got_b = swap(b[2:].astype(BF16), "row", 4)
    a, b = a[0::2] + got_a.astype(F32), b[:2] + got_b.astype(F32)
    got_a, bias = swap_with_bias(a[1].astype(BF16), bias, "row", 4)
    got_b = swap(b[1].astype(BF16), "row", 2)
    a, b = a[0] + got_a.astype(F32), b[0] + got_b.astype(F32)
    got, bias = swap_with_bias(jnp.stack([a[1], b[1]]).astype(BF16), bias, "col", 1)
    s = jnp.stack([a[0], b[0]]) + got.astype(F32)
    got, bias = swap_with_bias(s[1].astype(BF16), bias, "col", 2)
    s = s[0] + got.astype(F32)
    bit = HALVES
    while bit < lax.axis_size("row"):
        s = s.astype(BF16)
        got, bias = swap_with_bias(s, bias, "row", bit)
        s = s.astype(F32) + got.astype(F32)
        bit *= 2
    s = s.astype(BF16)
    s = jnp.stack([s, swap(s, "col", 2)])
    t = swap(s, "col", 1)
    a, b = jnp.stack([s[0], t[0]]), jnp.stack([s[1], t[1]])
    a, b = jnp.stack([a, swap(a, "row", 4)]), jnp.stack([b, swap(b, "row", 2)])
    far_a, far_b = swap(a, "row", 2), swap(b, "row", 4)
    a = jnp.stack([a, far_a], axis=1).reshape((4,) + a.shape[1:])
    b = jnp.concatenate([b, far_b])
    mine = jnp.concatenate([a, b], axis=1)
    return mine, swap(mine, "row", 1), bias


def local(x, cols, tw, ws, wn, bias_hidden, wo, bias_out, cot):
    rows, width = x.shape
    hidden = ws.shape[1]
    blocks, tile, depth = tw.shape
    both = ("row", "col")
    count = lax.axis_size(both)
    tile_scale = 0.25 / math.sqrt(depth)
    grad_scale = 1.0 / math.sqrt(rows * count)
    forward = [(i, i + 1) for i in range(count - 1)]
    backward = [(j, i) for i, j in forward]
    place = jnp.stack(
        [
            lax.axis_index(both) * blocks - blocks,
            lax.rem(lax.axis_index("row"), HALVES),
            lax.axis_index("col"),
        ]
    ).astype(jnp.int32)
    sds = jax.ShapeDtypeStruct
    low = lax.ppermute(x, both, forward)
    high = lax.ppermute(x, both, backward)
    adj, x_t, cot_t, wo_t, w_back, cot_sum = pl.pallas_call(
        functools.partial(prepare_kernel, tile_scale),
        out_shape=(
            sds((blocks, tile, depth), BF16),
            sds((width, rows), BF16),
            sds((width, rows), BF16),
            sds((width, hidden), BF16),
            sds((hidden, 2 * width), BF16),
            sds((1, width), F32),
        ),
        in_specs=[vmem()] * 6,
        out_specs=[vmem()] * 6,
        compiler_params=params(),
        cost_estimate=pl.CostEstimate(flops=4 * blocks * tile * depth, bytes_accessed=9 << 20, transcendentals=0),
        name="prepare",
    )(tw, x, cot, ws, wn, wo)
    piece = 3 * width // QUARTERS
    shape = (HALVES // 2, QUARTERS, piece, LANES)
    hid, dh, keep, send, hidden_sum = pl.pallas_call(
        forward_kernel,
        out_shape=(
            sds((rows, hidden), BF16),
            sds((rows, hidden), BF16),
            sds(shape, F32),
            sds(shape, BF16),
            sds((1, hidden), F32),
        ),
        in_specs=[smem(), smem()] + [vmem()] * 11,
        out_specs=[vmem()] * 5,
        scratch_shapes=[
            pltpu.VMEM((3 * rows, width), BF16),
            pltpu.VMEM((rows, width), BF16),
            pltpu.VMEM((2 * width, rows), BF16),
        ],
        compiler_params=params(),
        cost_estimate=pl.CostEstimate(
            flops=2 * rows * width * (6 * hidden + depth), bytes_accessed=14 << 20, transcendentals=rows * hidden
        ),
        name="forward",
    )(place, cols, low, x, high, adj, x_t, cot, cot_t, ws, wn, bias_hidden.reshape(1, -1), wo_t)
    embed, own, to_low, to_high = pl.pallas_call(
        backward_kernel,
        out_shape=(
            sds((rows, width), BF16),
            sds((rows, width), F32),
            sds((rows, width), BF16),
            sds((rows, width), BF16),
        ),
        in_specs=[smem(), smem()] + [vmem()] * 6,
        out_specs=[vmem()] * 4,
        scratch_shapes=[pltpu.VMEM((3 * rows, width), F32), pltpu.VMEM((rows, width), BF16)],
        compiler_params=params(),
        cost_estimate=pl.CostEstimate(
            flops=2 * rows * width * (3 * hidden + depth), bytes_accessed=10 << 20, transcendentals=0
        ),
        name="backward",
    )(place, cols, adj, hid, dh, wo, bias_out.reshape(1, -1), w_back)
    from_high = lax.ppermute(to_low, both, backward)
    from_low = lax.ppermute(to_high, both, forward)
    grad_features = (own + from_low.astype(F32) + from_high.astype(F32)).astype(BF16)
    bias = jnp.concatenate([hidden_sum.reshape(-1, width), cot_sum])
    bias = jnp.pad(bias, ((0, 8 - bias.shape[0]), (0, 0)))
    mine, other, bias = all_reduce(keep, send, bias)
    g_self, g_neigh, g_out = pl.pallas_call(
        functools.partial(unpack_kernel, grad_scale),
        out_shape=(sds((width, hidden), F32), sds((width, hidden), F32), sds((hidden, width), F32)),
        in_specs=[smem(), vmem(), vmem()],
        out_specs=[vmem()] * 3,
        scratch_shapes=[pltpu.VMEM((width, LANES), F32)],
        compiler_params=params(),
        cost_estimate=pl.CostEstimate(flops=3 * width * hidden, bytes_accessed=9 * width * hidden, transcendentals=0),
        name="unpack",
    )(place, mine, other)
    bias = bias * grad_scale
    top = hidden // width
    return embed, grad_features, g_self, g_neigh, bias[:top].reshape(-1), g_out, bias[top]


def solution(mesh):
    share = P(("row", "col"), None)
    in_specs = (share, share, P(("row", "col"), None, None), P(), P(), P(), P(), P(), share)
    out_specs = (share, share, P(), P(), P(), P(), P())
    return jax.shard_map(local, mesh=mesh, in_specs=in_specs, out_specs=out_specs, check_vma=False)
```

```python
import functools
import math

import jax
import jax.numpy as jnp
from jax import lax
from jax.experimental import pallas as pl
from jax.experimental.pallas import tpu as pltpu
from jax.sharding import PartitionSpec as P

BF16 = jnp.bfloat16
F32 = jnp.float32
GELU_C = math.sqrt(2.0 / math.pi)
GELU_A = 0.044715
LANES = 128
HALVES = 8
QUARTERS = 4
BIAS_ROWS = 16


def vmem():
    return pl.BlockSpec(memory_space=pltpu.VMEM)


def smem():
    return pl.BlockSpec(memory_space=pltpu.SMEM)


def params(mib):
    return pltpu.CompilerParams(vmem_limit_bytes=mib * 1024 * 1024)


def dot(a, b):
    return jnp.dot(a, b, preferred_element_type=F32)


def prepare_kernel(
    tile_scale, tw, x, cot, ws, wn, wo, bias, adj, x_t, cot_t, wn_t, ws_t, pre, half_act, bias_sum
):
    rows, width = x.shape
    for b in range(tw.shape[0]):
        adj[b] = (tw[b].astype(F32) * tile_scale).astype(BF16)
    x_t[...] = x[...].T
    cot_t[...] = cot[...].T
    wn_t[...] = wn[...].T
    ws_t[...] = ws[...].T
    bias_sum[...] = jnp.sum(cot[...].astype(F32), axis=0, keepdims=True)
    wo_t = wo[...].T
    step = 256
    for r in range(0, rows, step):
        pre[r : r + step] = dot(x[r : r + step], ws[...]) + bias[...]
        half_act[r : r + step] = dot(cot[r : r + step], wo_t) * 0.5


def forward_kernel(
    place, cols, lo, x, hi, adj, x_t, cot_t, wn, pre, half_act, cot_sum, hid, dh, keep, send, bias,
    window, agg, left, sums
):
    rows, width = x.shape
    hidden = wn.shape[1]
    blocks, tile, _ = adj.shape
    slots = cols.shape[1]
    first, me, z = place[0], place[1], place[2]
    window[:rows] = lo[...]
    window[rows : 2 * rows] = x[...]
    window[2 * rows :] = hi[...]
    for b in range(blocks):
        parts = []
        for s in range(slots):
            at = pl.multiple_of((cols[b, s] - first) * tile, tile)
            parts.append(window[pl.ds(at, tile), :])
        agg[b * tile : (b + 1) * tile, :] = dot(adj[b], jnp.concatenate(parts, axis=0)).astype(BF16)
    left[:width] = x_t[...]
    left[width : 2 * width] = agg[...].T
    left[2 * width :] = jnp.ones((BIAS_ROWS, rows), BF16)
    chunk = 2 * LANES
    piece = width // QUARTERS
    core = lax.rem(me, 2)
    pair = me // 2
    sums[...] = jnp.zeros(sums.shape, F32)
    step = 256
    for c in range(hidden // chunk):
        at = slice(c * chunk, (c + 1) * chunk)
        for r in range(0, rows, step):
            sl = slice(r, r + step)
            v = dot(agg[sl], wn[:, at]) + pre[sl, at]
            sq = v * v
            t = jnp.tanh(v * (GELU_C + (GELU_C * GELU_A) * sq))
            h = 1.0 + t
            p = v * h
            hid[sl, at] = (0.5 * p).astype(BF16)
            slope = h + p * (GELU_C + (3.0 * GELU_C * GELU_A) * sq) * (1.0 - t)
            dh[sl, at] = (half_act[sl, at] * slope).astype(BF16)
        g = dot(left[...], dh[:, at])
        g_out = dot(cot_t[...], hid[:, at])
        for half in range(2):
            sums[2 * c + half : 2 * c + half + 1] = g[2 * width : 2 * width + 1, half * LANES : (half + 1) * LANES]
        base = jnp.bitwise_xor(c, pair) * QUARTERS
        for t, value in enumerate((g[:width], g[width : 2 * width], g_out)):
            mine = jnp.where(core == 0, value[:, :LANES], value[:, LANES:])
            other = jnp.where(core == 0, value[:, LANES:], value[:, :LANES]).astype(BF16)
            for k in range(QUARTERS):
                to = pl.multiple_of((base + jnp.bitwise_xor(k, z)) * (3 * piece) + t * piece, piece)
                keep[pl.ds(to, piece)] = mine[k * piece : (k + 1) * piece]
                send[pl.ds(to, piece)] = other[k * piece : (k + 1) * piece]
    top = hidden // LANES
    for i in range(width // LANES):
        sums[top + i : top + i + 1] = cot_sum[:, i * LANES : (i + 1) * LANES]
    high = sums[...].astype(BF16)
    low = (sums[...] - high.astype(F32)).astype(BF16)
    bias[...] = high.astype(F32) + low.astype(F32)
    end = send.shape[0] - 2 * BIAS_ROWS
    send[end : end + BIAS_ROWS] = high
    send[end + BIAS_ROWS :] = low


def spread_kernel(place, cols, adj, dh, wn_t, own, to_low, to_high, total, d_agg):
    rows, width = own.shape
    blocks, tile, _ = adj.shape
    slots = cols.shape[1]
    first = place[0]
    step = 256
    for r in range(0, rows, step):
        d_agg[r : r + step] = dot(dh[r : r + step], wn_t[...]).astype(BF16)
    total[...] = jnp.zeros(total.shape, F32)
    for b in range(blocks):
        spread = lax.dot_general(
            adj[b], d_agg[b * tile : (b + 1) * tile], (((0,), (0,)), ((), ())), preferred_element_type=F32
        )
        for s in range(slots):
            at = pl.multiple_of((cols[b, s] - first) * tile, tile)
            total[pl.ds(at, tile), :] += spread[s * tile : (s + 1) * tile]
    to_low[...] = total[:rows].astype(BF16)
    to_high[...] = total[2 * rows :].astype(BF16)
    own[...] = total[rows : 2 * rows]


def finish_kernel(hid, dh, wo, bias_out, ws_t, own, embed, near):
    rows = embed.shape[0]
    step = 256
    for r in range(0, rows, step):
        sl = slice(r, r + step)
        near[sl] = own[sl] + dot(dh[sl], ws_t[...])
        embed[sl] = (dot(hid[sl], wo[...]) + bias_out[...]).astype(BF16)


def unpack_kernel(scale, half, place, src, *refs):
    g_self, g_neigh, g_out, blocks, turned, flipped, sems = refs[-7:]
    width = g_self.shape[0]
    piece = width // QUARTERS
    me, z = place[1], place[2]
    copies = []
    for j in range(HALVES // 2):
        p = 2 * jnp.bitwise_xor(j, me // 2) + jnp.bitwise_xor(lax.rem(me, 2), half)
        at = pl.ds(pl.multiple_of(p * LANES, LANES), LANES)
        for k in range(QUARTERS):
            to = pl.ds(pl.multiple_of(jnp.bitwise_xor(k, z) * piece, piece), piece)
            blocks[0, j, to] = src[j, k, :piece].astype(F32) * scale
            blocks[1, j, to] = src[j, k, piece : 2 * piece].astype(F32) * scale
            turned[j, to] = src[j, k, 2 * piece :].astype(F32) * scale
        flipped[j] = turned[j].T
        copies.append(pltpu.make_async_copy(blocks.at[0, j], g_self.at[:, at], sems.at[j]))
        copies.append(pltpu.make_async_copy(blocks.at[1, j], g_neigh.at[:, at], sems.at[4 + j]))
        copies.append(pltpu.make_async_copy(flipped.at[j], g_out.at[at], sems.at[8 + j]))
        for copy in copies[-3:]:
            copy.start()
    for copy in copies:
        copy.wait()


def unpack(scale, half, place, src, width, hidden, before=()):
    sds = jax.ShapeDtypeStruct
    anywhere = pl.BlockSpec(memory_space=pl.ANY)
    return pl.pallas_call(
        functools.partial(unpack_kernel, scale, half),
        out_shape=(sds((width, hidden), F32), sds((width, hidden), F32), sds((hidden, width), F32)),
        in_specs=[smem(), vmem()] + [anywhere] * len(before),
        out_specs=[anywhere] * 3,
        input_output_aliases={2 + i: i for i in range(len(before))},
        scratch_shapes=[
            pltpu.VMEM((2, HALVES // 2, width, LANES), F32),
            pltpu.VMEM((HALVES // 2, width, LANES), F32),
            pltpu.VMEM((HALVES // 2, LANES, width), F32),
            pltpu.SemaphoreType.DMA((12,)),
        ],
        compiler_params=params(8),
        cost_estimate=pl.CostEstimate(flops=2 * width * hidden, bytes_accessed=9 * width * hidden, transcendentals=0),
        name="unpack",
    )(place, src, *before)


def swap(value, axis, bit):
    return lax.ppermute(value, axis, [(i, i ^ bit) for i in range(lax.axis_size(axis))])


def swap_with_bias(value, bias, axis, bit):
    high = lax.reduce_precision(bias, 8, 7)
    low = lax.reduce_precision(bias - high, 8, 7)
    message = jnp.concatenate([value.reshape(-1, LANES), high.astype(BF16), low.astype(BF16)])
    got, theirs = received(swap(message, axis, bit), value.shape)
    return got, (high + low) + theirs


def received(message, shape):
    end = message.shape[0] - 2 * BIAS_ROWS
    bias = message[end : end + BIAS_ROWS].astype(F32) + message[end + BIAS_ROWS :].astype(F32)
    return message[:end].reshape(shape), bias


def reduce_first(keep, send, bias):
    shape = (HALVES // 2, QUARTERS, -1, LANES)
    got, theirs = received(swap(send, "row", 1), keep.shape)
    return (keep + got.astype(F32)).reshape(shape), bias + theirs


def reduce_among(parts, bias, axis, bits):
    high = lax.reduce_precision(bias, 8, 7)
    low = lax.reduce_precision(bias - high, 8, 7)
    extra = [high.astype(BF16), low.astype(BF16)]
    shape = parts[0].shape
    one, two, three = [
        received(swap(jnp.concatenate([v.astype(BF16).reshape(-1, LANES)] + extra), axis, bit), shape)
        for v, bit in zip(parts[1:], bits)
    ]
    total = (parts[0] + one[0].astype(F32)) + (two[0].astype(F32) + three[0].astype(F32))
    return total, ((high + low) + one[1]) + (two[1] + three[1])


def reduce_far(s, bias):
    bit = HALVES
    while bit < lax.axis_size("row"):
        s = s.astype(BF16)
        got, bias = swap_with_bias(s, bias, "row", bit)
        s = s.astype(F32) + got.astype(F32)
        bit *= 2
    return s.astype(BF16), bias


def gather_among(s, axis, bits):
    return jnp.stack([s] + [swap(s, axis, bit) for bit in bits])


def gather_plane(s):
    a, b = s[:2], s[2:]
    a, b = jnp.stack([a, swap(a, "row", 4)]), jnp.stack([b, swap(b, "row", 2)])
    far_a, far_b = swap(a, "row", 2), swap(b, "row", 4)
    a = jnp.stack([a, far_a], axis=1).reshape((4,) + a.shape[1:])
    b = jnp.concatenate([b, far_b])
    return jnp.concatenate([a, b], axis=1)


def local(x, cols, tw, ws, wn, bias_hidden, wo, bias_out, cot):
    rows, width = x.shape
    hidden = ws.shape[1]
    blocks, tile, depth = tw.shape
    both = ("row", "col")
    count = lax.axis_size(both)
    tile_scale = 0.25 / math.sqrt(depth)
    grad_scale = 1.0 / math.sqrt(rows * count)
    forward = [(i, i + 1) for i in range(count - 1)]
    backward = [(j, i) for i, j in forward]
    place = jnp.stack(
        [
            lax.axis_index(both) * blocks - blocks,
            lax.rem(lax.axis_index("row"), HALVES),
            lax.axis_index("col"),
        ]
    ).astype(jnp.int32)
    sds = jax.ShapeDtypeStruct
    low = lax.ppermute(x, both, forward)
    high = lax.ppermute(x, both, backward)
    adj, x_t, cot_t, wn_t, ws_t, pre, half_act, cot_sum = pl.pallas_call(
        functools.partial(prepare_kernel, tile_scale),
        out_shape=(
            sds((blocks, tile, depth), BF16),
            sds((width, rows), BF16),
            sds((width, rows), BF16),
            sds((hidden, width), BF16),
            sds((hidden, width), BF16),
            sds((rows, hidden), F32),
            sds((rows, hidden), F32),
            sds((1, width), F32),
        ),
        in_specs=[vmem()] * 7,
        out_specs=[vmem()] * 8,
        compiler_params=params(22),
        cost_estimate=pl.CostEstimate(flops=4 * rows * width * hidden, bytes_accessed=9 << 20, transcendentals=0),
        name="prepare",
    )(tw, x, cot, ws, wn, wo, bias_hidden.reshape(1, -1))
    size = HALVES // 2 * 3 * width
    hid, dh, keep, send, bias = pl.pallas_call(
        forward_kernel,
        out_shape=(
            sds((rows, hidden), BF16),
            sds((rows, hidden), BF16),
            sds((size, LANES), F32),
            sds((size + 2 * BIAS_ROWS, LANES), BF16),
            sds((BIAS_ROWS, LANES), F32),
        ),
        in_specs=[smem(), smem()] + [vmem()] * 10,
        out_specs=[vmem()] * 5,
        scratch_shapes=[
            pltpu.VMEM((3 * rows, width), BF16),
            pltpu.VMEM((rows, width), BF16),
            pltpu.VMEM((2 * width + BIAS_ROWS, rows), BF16),
            pltpu.VMEM((BIAS_ROWS, LANES), F32),
        ],
        compiler_params=params(30),
        cost_estimate=pl.CostEstimate(
            flops=2 * rows * width * (4 * hidden + depth), bytes_accessed=14 << 20, transcendentals=rows * hidden
        ),
        name="forward",
    )(place, cols, low, x, high, adj, x_t, cot_t, wn, pre, half_act, cot_sum)
    acc, bias = reduce_first(keep, send, bias)
    acc, dh = lax.optimization_barrier((acc, dh))
    own, to_low, to_high = pl.pallas_call(
        spread_kernel,
        out_shape=(sds((rows, width), F32), sds((rows, width), BF16), sds((rows, width), BF16)),
        in_specs=[smem(), smem()] + [vmem()] * 3,
        out_specs=[vmem()] * 3,
        scratch_shapes=[pltpu.VMEM((3 * rows, width), F32), pltpu.VMEM((rows, width), BF16)],
        compiler_params=params(16),
        cost_estimate=pl.CostEstimate(
            flops=2 * rows * width * (hidden + depth), bytes_accessed=6 << 20, transcendentals=0
        ),
        name="spread",
    )(place, cols, adj, dh, wn_t)
    acc, bias = reduce_among([acc[i] for i in range(4)], bias, "row", (2, 4, 6))
    acc, hid, dh, own = lax.optimization_barrier((acc, hid, dh, own))
    embed, own = pl.pallas_call(
        finish_kernel,
        out_shape=(sds((rows, width), BF16), sds((rows, width), F32)),
        in_specs=[vmem()] * 6,
        out_specs=[vmem()] * 2,
        compiler_params=params(12),
        cost_estimate=pl.CostEstimate(flops=4 * rows * width * hidden, bytes_accessed=8 << 20, transcendentals=0),
        name="finish",
    )(hid, dh, wo, bias_out.reshape(1, -1), ws_t, own)
    part, bias = reduce_among([acc[i] for i in range(4)], bias, "col", (1, 2, 3))
    part, to_low, to_high = lax.optimization_barrier((part, to_low, to_high))
    part, bias = reduce_far(part, bias)
    from_high = lax.ppermute(to_low, both, backward)
    from_low = lax.ppermute(to_high, both, forward)
    part = gather_among(part, "col", (1, 2, 3))
    mine = gather_plane(part)
    mine, from_high, from_low = lax.optimization_barrier((mine, from_high, from_low))
    other = swap(mine, "row", 1)
    grad_features = (own + from_low.astype(F32) + from_high.astype(F32)).astype(BF16)
    grads = unpack(grad_scale, 0, place, mine, width, hidden)
    g_self, g_neigh, g_out = unpack(grad_scale, 1, place, other, width, hidden, grads)
    bias = bias * grad_scale
    top = hidden // LANES
    bias_h, bias_o = bias[:top].reshape(-1), bias[top : top + width // LANES].reshape(-1)
    return embed, grad_features, g_self, g_neigh, bias_h, g_out, bias_o


def solution(mesh):
    share = P(("row", "col"), None)
    in_specs = (share, share, P(("row", "col"), None, None), P(), P(), P(), P(), P(), share)
    out_specs = (share, share, P(), P(), P(), P(), P())
    return jax.shard_map(local, mesh=mesh, in_specs=in_specs, out_specs=out_specs, check_vma=False)
```

```python
import functools
import math

import jax
import jax.numpy as jnp
from jax import lax
from jax.experimental import pallas as pl
from jax.experimental.pallas import tpu as pltpu
from jax.sharding import PartitionSpec as P

BF16 = jnp.bfloat16
F32 = jnp.float32
GELU_C = math.sqrt(2.0 / math.pi)
GELU_A = 0.044715
LANES = 128
HALVES = 8
QUARTERS = 4
BIAS_ROWS = 16


def vmem():
    return pl.BlockSpec(memory_space=pltpu.VMEM)


def smem():
    return pl.BlockSpec(memory_space=pltpu.SMEM)


def params(mib):
    return pltpu.CompilerParams(vmem_limit_bytes=mib * 1024 * 1024)


def dot(a, b):
    return jnp.dot(a, b, preferred_element_type=F32)


def prepare_kernel(
    tile_scale, tw, x, cot, ws, wn, wo, bias, adj, x_t, cot_t, wn_t, ws_t, pre, half_act, bias_sum
):
    rows, width = x.shape
    for b in range(tw.shape[0]):
        adj[b] = (tw[b].astype(F32) * tile_scale).astype(BF16)
    x_t[...] = x[...].T
    cot_t[...] = cot[...].T
    wn_t[...] = wn[...].T
    ws_t[...] = ws[...].T
    bias_sum[...] = jnp.sum(cot[...].astype(F32), axis=0, keepdims=True)
    wo_t = wo[...].T
    step = 256
    for r in range(0, rows, step):
        pre[r : r + step] = dot(x[r : r + step], ws[...]) + bias[...]
        half_act[r : r + step] = dot(cot[r : r + step], wo_t) * 0.5


def forward_kernel(
    place, cols, lo, x, hi, adj, x_t, cot_t, wn, pre, half_act, cot_sum, hid, dh, keep, send, bias,
    window, agg, left, sums
):
    rows, width = x.shape
    hidden = wn.shape[1]
    blocks, tile, _ = adj.shape
    slots = cols.shape[1]
    first, me, z = place[0], place[1], place[2]
    window[:rows] = lo[...]
    window[rows : 2 * rows] = x[...]
    window[2 * rows :] = hi[...]
    for b in range(blocks):
        parts = []
        for s in range(slots):
            at = pl.multiple_of((cols[b, s] - first) * tile, tile)
            parts.append(window[pl.ds(at, tile), :])
        agg[b * tile : (b + 1) * tile, :] = dot(adj[b], jnp.concatenate(parts, axis=0)).astype(BF16)
    left[:width] = x_t[...]
    left[width : 2 * width] = agg[...].T
    left[2 * width :] = jnp.ones((BIAS_ROWS, rows), BF16)
    chunk = 2 * LANES
    piece = width // QUARTERS
    core = lax.rem(me, 2)
    pair = me // 2
    sums[...] = jnp.zeros(sums.shape, F32)
    step = 256
    for c in range(hidden // chunk):
        at = slice(c * chunk, (c + 1) * chunk)
        for r in range(0, rows, step):
            sl = slice(r, r + step)
            v = dot(agg[sl], wn[:, at]) + pre[sl, at]
            sq = v * v
            t = jnp.tanh(v * (GELU_C + (GELU_C * GELU_A) * sq))
            h = 1.0 + t
            p = v * h
            hid[sl, at] = (0.5 * p).astype(BF16)
            slope = h + p * (GELU_C + (3.0 * GELU_C * GELU_A) * sq) * (1.0 - t)
            dh[sl, at] = (half_act[sl, at] * slope).astype(BF16)
        g = dot(left[...], dh[:, at])
        g_out = dot(cot_t[...], hid[:, at])
        for half in range(2):
            sums[2 * c + half : 2 * c + half + 1] = g[2 * width : 2 * width + 1, half * LANES : (half + 1) * LANES]
        base = jnp.bitwise_xor(c, pair) * QUARTERS
        for t, value in enumerate((g[:width], g[width : 2 * width], g_out)):
            mine = jnp.where(core == 0, value[:, :LANES], value[:, LANES:])
            other = jnp.where(core == 0, value[:, LANES:], value[:, :LANES]).astype(BF16)
            for k in range(QUARTERS):
                to = pl.multiple_of((base + jnp.bitwise_xor(k, z)) * (3 * piece) + t * piece, piece)
                keep[pl.ds(to, piece)] = mine[k * piece : (k + 1) * piece]
                send[pl.ds(to, piece)] = other[k * piece : (k + 1) * piece]
    top = hidden // LANES
    for i in range(width // LANES):
        sums[top + i : top + i + 1] = cot_sum[:, i * LANES : (i + 1) * LANES]
    high = sums[...].astype(BF16)
    low = (sums[...] - high.astype(F32)).astype(BF16)
    bias[...] = high.astype(F32) + low.astype(F32)
    end = send.shape[0] - 2 * BIAS_ROWS
    send[end : end + BIAS_ROWS] = high
    send[end + BIAS_ROWS :] = low


def spread_kernel(place, cols, adj, dh, wn_t, own, to_low, to_high, total, d_agg):
    rows, width = own.shape
    blocks, tile, _ = adj.shape
    slots = cols.shape[1]
    first = place[0]
    step = 256
    for r in range(0, rows, step):
        d_agg[r : r + step] = dot(dh[r : r + step], wn_t[...]).astype(BF16)
    total[...] = jnp.zeros(total.shape, F32)
    for b in range(blocks):
        spread = lax.dot_general(
            adj[b], d_agg[b * tile : (b + 1) * tile], (((0,), (0,)), ((), ())), preferred_element_type=F32
        )
        for s in range(slots):
            at = pl.multiple_of((cols[b, s] - first) * tile, tile)
            total[pl.ds(at, tile), :] += spread[s * tile : (s + 1) * tile]
    to_low[...] = total[:rows].astype(BF16)
    to_high[...] = total[2 * rows :].astype(BF16)
    own[...] = total[rows : 2 * rows]


def finish_kernel(hid, dh, wo, bias_out, ws_t, own, embed, near):
    rows = embed.shape[0]
    step = 256
    for r in range(0, rows, step):
        sl = slice(r, r + step)
        near[sl] = own[sl] + dot(dh[sl], ws_t[...])
        embed[sl] = (dot(hid[sl], wo[...]) + bias_out[...]).astype(BF16)


def place_grads(scale, half, place, src, outs, scratch):
    g_self, g_neigh, g_out = outs
    blocks, turned, flipped, sems = scratch
    width = g_self.shape[0]
    piece = width // QUARTERS
    me, z = place[1], place[2]
    copies = []
    for j in range(HALVES // 2):
        p = 2 * jnp.bitwise_xor(j, me // 2) + jnp.bitwise_xor(lax.rem(me, 2), half)
        at = pl.ds(pl.multiple_of(p * LANES, LANES), LANES)
        for k in range(QUARTERS):
            to = pl.ds(pl.multiple_of(jnp.bitwise_xor(k, z) * piece, piece), piece)
            blocks[0, j, to] = src[j, k, :piece].astype(F32) * scale
            blocks[1, j, to] = src[j, k, piece : 2 * piece].astype(F32) * scale
            turned[j, to] = src[j, k, 2 * piece :].astype(F32) * scale
        flipped[j] = turned[j].T
        copies.append(pltpu.make_async_copy(blocks.at[0, j], g_self.at[:, at], sems.at[j]))
        copies.append(pltpu.make_async_copy(blocks.at[1, j], g_neigh.at[:, at], sems.at[4 + j]))
        copies.append(pltpu.make_async_copy(flipped.at[j], g_out.at[at], sems.at[8 + j]))
        for copy in copies[-3:]:
            copy.start()
    return copies


def first_unpack_kernel(
    scale, place, src, own, from_low, from_high, bias,
    g_self, g_neigh, g_out, features, bias_hidden, bias_out, *scratch
):
    copies = place_grads(scale, 0, place, src, (g_self, g_neigh, g_out), scratch)
    features[...] = (own[...] + from_low[...].astype(F32) + from_high[...].astype(F32)).astype(BF16)
    top, count = bias_hidden.shape[0], bias_out.shape[0]
    bias_hidden[...] = bias[:top] * scale
    bias_out[...] = bias[top : top + count] * scale
    for copy in copies:
        copy.wait()


def second_unpack_kernel(scale, place, src, _0, _1, _2, g_self, g_neigh, g_out, *scratch):
    for copy in place_grads(scale, 1, place, src, (g_self, g_neigh, g_out), scratch):
        copy.wait()


def unpack_scratch(width):
    return [
        pltpu.VMEM((2, HALVES // 2, width, LANES), F32),
        pltpu.VMEM((HALVES // 2, width, LANES), F32),
        pltpu.VMEM((HALVES // 2, LANES, width), F32),
        pltpu.SemaphoreType.DMA((12,)),
    ]


def swap(value, axis, bit):
    return lax.ppermute(value, axis, [(i, i ^ bit) for i in range(lax.axis_size(axis))])


def swap_with_bias(value, bias, axis, bit):
    high = lax.reduce_precision(bias, 8, 7)
    low = lax.reduce_precision(bias - high, 8, 7)
    message = jnp.concatenate([value.reshape(-1, LANES), high.astype(BF16), low.astype(BF16)])
    got, theirs = received(swap(message, axis, bit), value.shape)
    return got, (high + low) + theirs


def received(message, shape):
    end = message.shape[0] - 2 * BIAS_ROWS
    bias = message[end : end + BIAS_ROWS].astype(F32) + message[end + BIAS_ROWS :].astype(F32)
    return message[:end].reshape(shape), bias


def reduce_first(keep, send, bias):
    shape = (HALVES // 2, QUARTERS, -1, LANES)
    got, theirs = received(swap(send, "row", 1), keep.shape)
    return (keep + got.astype(F32)).reshape(shape), bias + theirs


def reduce_among(parts, bias, axis, bits):
    high = lax.reduce_precision(bias, 8, 7)
    low = lax.reduce_precision(bias - high, 8, 7)
    extra = [high.astype(BF16), low.astype(BF16)]
    shape = parts[0].shape
    one, two, three = [
        received(swap(jnp.concatenate([v.astype(BF16).reshape(-1, LANES)] + extra), axis, bit), shape)
        for v, bit in zip(parts[1:], bits)
    ]
    total = (parts[0] + one[0].astype(F32)) + (two[0].astype(F32) + three[0].astype(F32))
    return total, ((high + low) + one[1]) + (two[1] + three[1])


def reduce_far(s, bias):
    bit = HALVES
    while bit < lax.axis_size("row"):
        s = s.astype(BF16)
        got, bias = swap_with_bias(s, bias, "row", bit)
        s = s.astype(F32) + got.astype(F32)
        bit *= 2
    return s.astype(BF16), bias


def gather_among(s, axis, bits):
    return jnp.stack([s] + [swap(s, axis, bit) for bit in bits])


def gather_near(s):
    a, b = s[:2], s[2:]
    return jnp.stack([a, swap(a, "row", 4)]), jnp.stack([b, swap(b, "row", 2)])


def gather_across(a, b):
    far_a, far_b = swap(a, "row", 2), swap(b, "row", 4)
    a = jnp.stack([a, far_a], axis=1).reshape((4,) + a.shape[1:])
    b = jnp.concatenate([b, far_b])
    return jnp.concatenate([a, b], axis=1)


def local(x, cols, tw, ws, wn, bias_hidden, wo, bias_out, cot):
    rows, width = x.shape
    hidden = ws.shape[1]
    blocks, tile, depth = tw.shape
    both = ("row", "col")
    count = lax.axis_size(both)
    tile_scale = 0.25 / math.sqrt(depth)
    grad_scale = 1.0 / math.sqrt(rows * count)
    forward = [(i, i + 1) for i in range(count - 1)]
    backward = [(j, i) for i, j in forward]
    place = jnp.stack(
        [
            lax.axis_index(both) * blocks - blocks,
            lax.rem(lax.axis_index("row"), HALVES),
            lax.axis_index("col"),
        ]
    ).astype(jnp.int32)
    sds = jax.ShapeDtypeStruct
    low = lax.ppermute(x, both, forward)
    high = lax.ppermute(x, both, backward)
    adj, x_t, cot_t, wn_t, ws_t, pre, half_act, cot_sum = pl.pallas_call(
        functools.partial(prepare_kernel, tile_scale),
        out_shape=(
            sds((blocks, tile, depth), BF16),
            sds((width, rows), BF16),
            sds((width, rows), BF16),
            sds((hidden, width), BF16),
            sds((hidden, width), BF16),
            sds((rows, hidden), F32),
            sds((rows, hidden), F32),
            sds((1, width), F32),
        ),
        in_specs=[vmem()] * 7,
        out_specs=[vmem()] * 8,
        compiler_params=params(22),
        cost_estimate=pl.CostEstimate(flops=4 * rows * width * hidden, bytes_accessed=9 << 20, transcendentals=0),
        name="prepare",
    )(tw, x, cot, ws, wn, wo, bias_hidden.reshape(1, -1))
    size = HALVES // 2 * 3 * width
    hid, dh, keep, send, bias = pl.pallas_call(
        forward_kernel,
        out_shape=(
            sds((rows, hidden), BF16),
            sds((rows, hidden), BF16),
            sds((size, LANES), F32),
            sds((size + 2 * BIAS_ROWS, LANES), BF16),
            sds((BIAS_ROWS, LANES), F32),
        ),
        in_specs=[smem(), smem()] + [vmem()] * 10,
        out_specs=[vmem()] * 5,
        scratch_shapes=[
            pltpu.VMEM((3 * rows, width), BF16),
            pltpu.VMEM((rows, width), BF16),
            pltpu.VMEM((2 * width + BIAS_ROWS, rows), BF16),
            pltpu.VMEM((BIAS_ROWS, LANES), F32),
        ],
        compiler_params=params(30),
        cost_estimate=pl.CostEstimate(
            flops=2 * rows * width * (4 * hidden + depth), bytes_accessed=14 << 20, transcendentals=rows * hidden
        ),
        name="forward",
    )(place, cols, low, x, high, adj, x_t, cot_t, wn, pre, half_act, cot_sum)
    acc, bias = reduce_first(keep, send, bias)
    acc, dh, hid = lax.optimization_barrier((acc, dh, hid))
    own, to_low, to_high = pl.pallas_call(
        spread_kernel,
        out_shape=(sds((rows, width), F32), sds((rows, width), BF16), sds((rows, width), BF16)),
        in_specs=[smem(), smem()] + [vmem()] * 3,
        out_specs=[vmem()] * 3,
        scratch_shapes=[pltpu.VMEM((3 * rows, width), F32), pltpu.VMEM((rows, width), BF16)],
        compiler_params=params(16),
        cost_estimate=pl.CostEstimate(
            flops=2 * rows * width * (hidden + depth), bytes_accessed=6 << 20, transcendentals=0
        ),
        name="spread",
    )(place, cols, adj, dh, wn_t)
    acc, bias = reduce_among([acc[i] for i in range(4)], bias, "row", (2, 4, 6))
    embed, own = pl.pallas_call(
        finish_kernel,
        out_shape=(sds((rows, width), BF16), sds((rows, width), F32)),
        in_specs=[vmem()] * 6,
        out_specs=[vmem()] * 2,
        compiler_params=params(12),
        cost_estimate=pl.CostEstimate(flops=4 * rows * width * hidden, bytes_accessed=8 << 20, transcendentals=0),
        name="finish",
    )(hid, dh, wo, bias_out.reshape(1, -1), ws_t, own)
    cut = 8 * rows // 16
    first = lax.ppermute(to_high[:cut], both, forward)
    acc, first, embed, own = lax.optimization_barrier((acc, first, embed, own))
    part, bias = reduce_among([acc[i] for i in range(4)], bias, "col", (1, 2, 3))
    part, to_low, to_high = lax.optimization_barrier((part, to_low, to_high))
    part, bias = reduce_far(part, bias)
    from_high = lax.ppermute(to_low, both, backward)
    last = lax.ppermute(to_high[cut:], both, forward)
    part = gather_among(part, "col", (1, 2, 3))
    a, b = gather_near(part)
    a, b, last = lax.optimization_barrier((a, b, last))
    mine = gather_across(a, b)
    mine, from_high = lax.optimization_barrier((mine, from_high))
    from_low = jnp.concatenate([first, last])
    other = swap(mine, "row", 1)
    anywhere = pl.BlockSpec(memory_space=pl.ANY)
    grads = (sds((width, hidden), F32), sds((width, hidden), F32), sds((hidden, width), F32))
    *grads_half, grad_features, bias_h, bias_o = pl.pallas_call(
        functools.partial(first_unpack_kernel, grad_scale),
        out_shape=grads
        + (sds((rows, width), BF16), sds((hidden // LANES, LANES), F32), sds((width // LANES, LANES), F32)),
        in_specs=[smem()] + [vmem()] * 5,
        out_specs=[anywhere] * 3 + [vmem()] * 3,
        scratch_shapes=unpack_scratch(width),
        compiler_params=params(10),
        cost_estimate=pl.CostEstimate(flops=4 * width * hidden, bytes_accessed=12 * width * hidden, transcendentals=0),
        name="first_unpack",
    )(place, mine, own, from_low, from_high, bias)
    g_self, g_neigh, g_out = pl.pallas_call(
        functools.partial(second_unpack_kernel, grad_scale),
        out_shape=grads,
        in_specs=[smem(), vmem()] + [anywhere] * 3,
        out_specs=[anywhere] * 3,
        input_output_aliases={2: 0, 3: 1, 4: 2},
        scratch_shapes=unpack_scratch(width),
        compiler_params=params(8),
        cost_estimate=pl.CostEstimate(flops=2 * width * hidden, bytes_accessed=9 * width * hidden, transcendentals=0),
        name="second_unpack",
    )(place, other, *grads_half)
    return embed, grad_features, g_self, g_neigh, bias_h.reshape(-1), g_out, bias_o.reshape(-1)


def solution(mesh):
    share = P(("row", "col"), None)
    in_specs = (share, share, P(("row", "col"), None, None), P(), P(), P(), P(), P(), share)
    out_specs = (share, share, P(), P(), P(), P(), P())
    return jax.shard_map(local, mesh=mesh, in_specs=in_specs, out_specs=out_specs, check_vma=False)
```

```python
import functools
import math

import jax
import jax.numpy as jnp
from jax import lax
from jax.experimental import pallas as pl
from jax.experimental.pallas import tpu as pltpu
from jax.sharding import PartitionSpec as P

BF16 = jnp.bfloat16
F32 = jnp.float32
GELU_C = math.sqrt(2.0 / math.pi)
GELU_A = 0.044715
LANES = 128
HALVES = 8
QUARTERS = 4
BIAS_ROWS = 16


def vmem():
    return pl.BlockSpec(memory_space=pltpu.VMEM)


def smem():
    return pl.BlockSpec(memory_space=pltpu.SMEM)


def params(mib):
    return pltpu.CompilerParams(vmem_limit_bytes=mib * 1024 * 1024)


def dot(a, b):
    return jnp.dot(a, b, preferred_element_type=F32)


def prepare_kernel(
    tile_scale, tw, x, cot, ws, wn, wo, bias, adj, x_t, cot_t, wn_t, ws_t, pre, half_act, bias_sum
):
    rows, width = x.shape
    for b in range(tw.shape[0]):
        adj[b] = (tw[b].astype(F32) * tile_scale).astype(BF16)
    x_t[...] = x[...].T
    cot_t[...] = cot[...].T
    wn_t[...] = wn[...].T
    ws_t[...] = ws[...].T
    bias_sum[...] = jnp.sum(cot[...].astype(F32), axis=0, keepdims=True)
    wo_t = wo[...].T
    step = 256
    for r in range(0, rows, step):
        pre[r : r + step] = dot(x[r : r + step], ws[...]) + bias[...]
        half_act[r : r + step] = dot(cot[r : r + step], wo_t) * 0.5


def forward_kernel(
    place, cols, lo, x, hi, adj, x_t, cot_t, wn, pre, half_act, cot_sum, hid, dh, keep, send, bias,
    window, agg, left, sums
):
    rows, width = x.shape
    hidden = wn.shape[1]
    blocks, tile, _ = adj.shape
    slots = cols.shape[1]
    first, me, z = place[0], place[1], place[2]
    window[:rows] = lo[...]
    window[rows : 2 * rows] = x[...]
    window[2 * rows :] = hi[...]
    for b in range(blocks):
        parts = []
        for s in range(slots):
            at = pl.multiple_of((cols[b, s] - first) * tile, tile)
            parts.append(window[pl.ds(at, tile), :])
        agg[b * tile : (b + 1) * tile, :] = dot(adj[b], jnp.concatenate(parts, axis=0)).astype(BF16)
    left[:width] = x_t[...]
    left[width : 2 * width] = agg[...].T
    left[2 * width :] = jnp.ones((BIAS_ROWS, rows), BF16)
    chunk = 2 * LANES
    piece = width // QUARTERS
    core = lax.rem(me, 2)
    pair = me // 2
    sums[...] = jnp.zeros(sums.shape, F32)
    step = 512
    for c in range(hidden // chunk):
        at = slice(c * chunk, (c + 1) * chunk)
        for r in range(0, rows, step):
            sl = slice(r, r + step)
            v = dot(agg[sl], wn[:, at]) + pre[sl, at]
            sq = v * v
            t = jnp.tanh(v * (GELU_C + (GELU_C * GELU_A) * sq))
            h = 1.0 + t
            p = v * h
            hid[sl, at] = (0.5 * p).astype(BF16)
            slope = h + p * (GELU_C + (3.0 * GELU_C * GELU_A) * sq) * (1.0 - t)
            dh[sl, at] = (half_act[sl, at] * slope).astype(BF16)
        g = dot(left[...], dh[:, at])
        g_out = dot(cot_t[...], hid[:, at])
        for half in range(2):
            sums[2 * c + half : 2 * c + half + 1] = g[2 * width : 2 * width + 1, half * LANES : (half + 1) * LANES]
        base = jnp.bitwise_xor(c, pair) * QUARTERS
        for t, value in enumerate((g[:width], g[width : 2 * width], g_out)):
            mine = jnp.where(core == 0, value[:, :LANES], value[:, LANES:])
            other = jnp.where(core == 0, value[:, LANES:], value[:, :LANES]).astype(BF16)
            for k in range(QUARTERS):
                to = pl.multiple_of((base + jnp.bitwise_xor(k, z)) * (3 * piece) + t * piece, piece)
                keep[pl.ds(to, piece)] = mine[k * piece : (k + 1) * piece]
                send[pl.ds(to, piece)] = other[k * piece : (k + 1) * piece]
    top = hidden // LANES
    for i in range(width // LANES):
        sums[top + i : top + i + 1] = cot_sum[:, i * LANES : (i + 1) * LANES]
    high = sums[...].astype(BF16)
    low = (sums[...] - high.astype(F32)).astype(BF16)
    bias[...] = high.astype(F32) + low.astype(F32)
    end = send.shape[0] - 2 * BIAS_ROWS
    send[end : end + BIAS_ROWS] = high
    send[end + BIAS_ROWS :] = low


def spread_kernel(place, cols, adj, dh, wn_t, own, to_low, to_high, total, d_agg):
    rows, width = own.shape
    blocks, tile, _ = adj.shape
    slots = cols.shape[1]
    first = place[0]
    step = 256
    for r in range(0, rows, step):
        d_agg[r : r + step] = dot(dh[r : r + step], wn_t[...]).astype(BF16)
    total[...] = jnp.zeros(total.shape, F32)
    for b in range(blocks):
        spread = lax.dot_general(
            adj[b], d_agg[b * tile : (b + 1) * tile], (((0,), (0,)), ((), ())), preferred_element_type=F32
        )
        for s in range(slots):
            at = pl.multiple_of((cols[b, s] - first) * tile, tile)
            total[pl.ds(at, tile), :] += spread[s * tile : (s + 1) * tile]
    to_low[...] = total[:rows].astype(BF16)
    to_high[...] = total[2 * rows :].astype(BF16)
    own[...] = total[rows : 2 * rows]


def finish_kernel(hid, dh, wo, bias_out, ws_t, own, embed, near):
    rows = embed.shape[0]
    step = 256
    for r in range(0, rows, step):
        sl = slice(r, r + step)
        near[sl] = own[sl] + dot(dh[sl], ws_t[...])
        embed[sl] = (dot(hid[sl], wo[...]) + bias_out[...]).astype(BF16)


def place_grads(scale, half, place, src, outs, scratch):
    g_self, g_neigh, g_out = outs
    blocks, turned, flipped, sems = scratch
    width = g_self.shape[0]
    piece = width // QUARTERS
    me, z = place[1], place[2]
    copies = []
    for j in range(HALVES // 2):
        p = 2 * jnp.bitwise_xor(j, me // 2) + jnp.bitwise_xor(lax.rem(me, 2), half)
        at = pl.ds(pl.multiple_of(p * LANES, LANES), LANES)
        for k in range(QUARTERS):
            to = pl.ds(pl.multiple_of(jnp.bitwise_xor(k, z) * piece, piece), piece)
            blocks[0, j, to] = src[j, k, :piece].astype(F32) * scale
            blocks[1, j, to] = src[j, k, piece : 2 * piece].astype(F32) * scale
            turned[j, to] = src[j, k, 2 * piece :].astype(F32) * scale
        flipped[j] = turned[j].T
        copies.append(pltpu.make_async_copy(blocks.at[0, j], g_self.at[:, at], sems.at[j]))
        copies.append(pltpu.make_async_copy(blocks.at[1, j], g_neigh.at[:, at], sems.at[4 + j]))
        copies.append(pltpu.make_async_copy(flipped.at[j], g_out.at[at], sems.at[8 + j]))
        for copy in copies[-3:]:
            copy.start()
    return copies


def first_unpack_kernel(
    scale, place, src, own, from_low, from_high, bias,
    g_self, g_neigh, g_out, features, bias_hidden, bias_out, *scratch
):
    summed, done, *scratch = scratch
    summed[...] = (own[...] + from_low[...].astype(F32) + from_high[...].astype(F32)).astype(BF16)
    store = pltpu.make_async_copy(summed, features, done)
    store.start()
    copies = place_grads(scale, 0, place, src, (g_self, g_neigh, g_out), scratch)
    top, count = bias_hidden.shape[0], bias_out.shape[0]
    bias_hidden[...] = bias[:top] * scale
    bias_out[...] = bias[top : top + count] * scale
    for copy in copies:
        copy.wait()
    store.wait()


def second_unpack_kernel(scale, place, src, _0, _1, _2, g_self, g_neigh, g_out, *scratch):
    for copy in place_grads(scale, 1, place, src, (g_self, g_neigh, g_out), scratch):
        copy.wait()


def unpack_scratch(width):
    return [
        pltpu.VMEM((2, HALVES // 2, width, LANES), F32),
        pltpu.VMEM((HALVES // 2, width, LANES), F32),
        pltpu.VMEM((HALVES // 2, LANES, width), F32),
        pltpu.SemaphoreType.DMA((12,)),
    ]


def swap(value, axis, bit):
    return lax.ppermute(value, axis, [(i, i ^ bit) for i in range(lax.axis_size(axis))])


def swap_with_bias(value, bias, axis, bit):
    high = lax.reduce_precision(bias, 8, 7)
    low = lax.reduce_precision(bias - high, 8, 7)
    message = jnp.concatenate([value.reshape(-1, LANES), high.astype(BF16), low.astype(BF16)])
    got, theirs = received(swap(message, axis, bit), value.shape)
    return got, (high + low) + theirs


def received(message, shape):
    end = message.shape[0] - 2 * BIAS_ROWS
    bias = message[end : end + BIAS_ROWS].astype(F32) + message[end + BIAS_ROWS :].astype(F32)
    return message[:end].reshape(shape), bias


def reduce_first(keep, send, bias):
    shape = (HALVES // 2, QUARTERS, -1, LANES)
    got, theirs = received(swap(send, "row", 1), keep.shape)
    return (keep + got.astype(F32)).reshape(shape), bias + theirs


def reduce_among(parts, bias, axis, bits):
    high = lax.reduce_precision(bias, 8, 7)
    low = lax.reduce_precision(bias - high, 8, 7)
    extra = [high.astype(BF16), low.astype(BF16)]
    shape = parts[0].shape
    one, two, three = [
        received(swap(jnp.concatenate([v.astype(BF16).reshape(-1, LANES)] + extra), axis, bit), shape)
        for v, bit in zip(parts[1:], bits)
    ]
    total = (parts[0] + one[0].astype(F32)) + (two[0].astype(F32) + three[0].astype(F32))
    return total, ((high + low) + one[1]) + (two[1] + three[1])


def reduce_far(s, bias):
    bit = HALVES
    while bit < lax.axis_size("row"):
        s = s.astype(BF16)
        got, bias = swap_with_bias(s, bias, "row", bit)
        s = s.astype(F32) + got.astype(F32)
        bit *= 2
    return s.astype(BF16), bias


def gather_among(s, axis, bits):
    return jnp.stack([s] + [swap(s, axis, bit) for bit in bits])


def gather_near(s):
    a, b = s[:2], s[2:]
    return jnp.stack([a, swap(a, "row", 4)]), jnp.stack([b, swap(b, "row", 2)])


def gather_across(a, b):
    far_a, far_b = swap(a, "row", 2), swap(b, "row", 4)
    a = jnp.stack([a, far_a], axis=1).reshape((4,) + a.shape[1:])
    b = jnp.concatenate([b, far_b])
    return jnp.concatenate([a, b], axis=1)


def local(x, cols, tw, ws, wn, bias_hidden, wo, bias_out, cot):
    rows, width = x.shape
    hidden = ws.shape[1]
    blocks, tile, depth = tw.shape
    both = ("row", "col")
    count = lax.axis_size(both)
    tile_scale = 0.25 / math.sqrt(depth)
    grad_scale = 1.0 / math.sqrt(rows * count)
    forward = [(i, i + 1) for i in range(count - 1)]
    backward = [(j, i) for i, j in forward]
    place = jnp.stack(
        [
            lax.axis_index(both) * blocks - blocks,
            lax.rem(lax.axis_index("row"), HALVES),
            lax.axis_index("col"),
        ]
    ).astype(jnp.int32)
    sds = jax.ShapeDtypeStruct
    low = lax.ppermute(x, both, forward)
    high = lax.ppermute(x, both, backward)
    adj, x_t, cot_t, wn_t, ws_t, pre, half_act, cot_sum = pl.pallas_call(
        functools.partial(prepare_kernel, tile_scale),
        out_shape=(
            sds((blocks, tile, depth), BF16),
            sds((width, rows), BF16),
            sds((width, rows), BF16),
            sds((hidden, width), BF16),
            sds((hidden, width), BF16),
            sds((rows, hidden), F32),
            sds((rows, hidden), F32),
            sds((1, width), F32),
        ),
        in_specs=[vmem()] * 7,
        out_specs=[vmem()] * 8,
        compiler_params=params(22),
        cost_estimate=pl.CostEstimate(flops=4 * rows * width * hidden, bytes_accessed=9 << 20, transcendentals=0),
        name="prepare",
    )(tw, x, cot, ws, wn, wo, bias_hidden.reshape(1, -1))
    size = HALVES // 2 * 3 * width
    hid, dh, keep, send, bias = pl.pallas_call(
        forward_kernel,
        out_shape=(
            sds((rows, hidden), BF16),
            sds((rows, hidden), BF16),
            sds((size, LANES), F32),
            sds((size + 2 * BIAS_ROWS, LANES), BF16),
            sds((BIAS_ROWS, LANES), F32),
        ),
        in_specs=[smem(), smem()] + [vmem()] * 10,
        out_specs=[vmem()] * 5,
        scratch_shapes=[
            pltpu.VMEM((3 * rows, width), BF16),
            pltpu.VMEM((rows, width), BF16),
            pltpu.VMEM((2 * width + BIAS_ROWS, rows), BF16),
            pltpu.VMEM((BIAS_ROWS, LANES), F32),
        ],
        compiler_params=params(30),
        cost_estimate=pl.CostEstimate(
            flops=2 * rows * width * (4 * hidden + depth), bytes_accessed=14 << 20, transcendentals=rows * hidden
        ),
        name="forward",
    )(place, cols, low, x, high, adj, x_t, cot_t, wn, pre, half_act, cot_sum)
    acc, bias = reduce_first(keep, send, bias)
    acc, dh, hid = lax.optimization_barrier((acc, dh, hid))
    own, to_low, to_high = pl.pallas_call(
        spread_kernel,
        out_shape=(sds((rows, width), F32), sds((rows, width), BF16), sds((rows, width), BF16)),
        in_specs=[smem(), smem()] + [vmem()] * 3,
        out_specs=[vmem()] * 3,
        scratch_shapes=[pltpu.VMEM((3 * rows, width), F32), pltpu.VMEM((rows, width), BF16)],
        compiler_params=params(16),
        cost_estimate=pl.CostEstimate(
            flops=2 * rows * width * (hidden + depth), bytes_accessed=6 << 20, transcendentals=0
        ),
        name="spread",
    )(place, cols, adj, dh, wn_t)
    acc, bias = reduce_among([acc[i] for i in range(4)], bias, "row", (2, 4, 6))
    end = 6 * rows // 16
    acc, hid, dh, own = lax.optimization_barrier((acc, hid, dh, own))
    embed, own = pl.pallas_call(
        finish_kernel,
        out_shape=(sds((rows, width), BF16), sds((rows, width), F32)),
        in_specs=[vmem()] * 6,
        out_specs=[vmem()] * 2,
        compiler_params=params(12),
        cost_estimate=pl.CostEstimate(flops=4 * rows * width * hidden, bytes_accessed=8 << 20, transcendentals=0),
        name="finish",
    )(hid, dh, wo, bias_out.reshape(1, -1), ws_t, own)
    part, bias = reduce_among([acc[i] for i in range(4)], bias, "col", (1, 2, 3))
    second = lax.ppermute(to_high[0:end], both, forward)
    part, second, to_low, to_high, embed, own = lax.optimization_barrier((part, second, to_low, to_high, embed, own))
    part, bias = reduce_far(part, bias)
    from_high = lax.ppermute(to_low, both, backward)
    last = lax.ppermute(to_high[end:], both, forward)
    part = gather_among(part, "col", (1, 2, 3))
    a, b = gather_near(part)
    a, b, last = lax.optimization_barrier((a, b, last))
    mine = gather_across(a, b)
    mine, from_high = lax.optimization_barrier((mine, from_high))
    from_low = jnp.concatenate([second, last])
    other = swap(mine, "row", 1)
    anywhere = pl.BlockSpec(memory_space=pl.ANY)
    grads = (sds((width, hidden), F32), sds((width, hidden), F32), sds((hidden, width), F32))
    *grads_half, grad_features, bias_h, bias_o = pl.pallas_call(
        functools.partial(first_unpack_kernel, grad_scale),
        out_shape=grads
        + (sds((rows, width), BF16), sds((hidden // LANES, LANES), F32), sds((width // LANES, LANES), F32)),
        in_specs=[smem()] + [vmem()] * 5,
        out_specs=[anywhere] * 4 + [vmem()] * 2,
        scratch_shapes=[pltpu.VMEM((rows, width), BF16), pltpu.SemaphoreType.DMA] + unpack_scratch(width),
        compiler_params=params(10),
        cost_estimate=pl.CostEstimate(flops=4 * width * hidden, bytes_accessed=12 * width * hidden, transcendentals=0),
        name="first_unpack",
    )(place, mine, own, from_low, from_high, bias)
    g_self, g_neigh, g_out = pl.pallas_call(
        functools.partial(second_unpack_kernel, grad_scale),
        out_shape=grads,
        in_specs=[smem(), vmem()] + [anywhere] * 3,
        out_specs=[anywhere] * 3,
        input_output_aliases={2: 0, 3: 1, 4: 2},
        scratch_shapes=unpack_scratch(width),
        compiler_params=params(8),
        cost_estimate=pl.CostEstimate(flops=2 * width * hidden, bytes_accessed=9 * width * hidden, transcendentals=0),
        name="second_unpack",
    )(place, other, *grads_half)
    return embed, grad_features, g_self, g_neigh, bias_h.reshape(-1), g_out, bias_o.reshape(-1)


def solution(mesh):
    share = P(("row", "col"), None)
    in_specs = (share, share, P(("row", "col"), None, None), P(), P(), P(), P(), P(), share)
    out_specs = (share, share, P(), P(), P(), P(), P())
    return jax.shard_map(local, mesh=mesh, in_specs=in_specs, out_specs=out_specs, check_vma=False)
```

```python
import functools
import math

import jax
import jax.numpy as jnp
from jax import lax
from jax.experimental import pallas as pl
from jax.experimental.pallas import tpu as pltpu
from jax.sharding import PartitionSpec as P

BF16 = jnp.bfloat16
F32 = jnp.float32
GELU_C = math.sqrt(2.0 / math.pi)
GELU_A = 0.044715
LANES = 128
HALVES = 8
QUARTERS = 4
BIAS_ROWS = 16


def vmem():
    return pl.BlockSpec(memory_space=pltpu.VMEM)


def smem():
    return pl.BlockSpec(memory_space=pltpu.SMEM)


def params(mib):
    return pltpu.CompilerParams(vmem_limit_bytes=mib * 1024 * 1024)


def dot(a, b):
    return jnp.dot(a, b, preferred_element_type=F32)


def prepare_kernel(
    tile_scale, tw, x, cot, ws, wn, wo, bias, adj, x_t, cot_t, wn_t, ws_t, pre, half_act, bias_sum
):
    rows, width = x.shape
    for b in range(tw.shape[0]):
        adj[b] = (tw[b].astype(F32) * tile_scale).astype(BF16)
    x_t[...] = x[...].T
    cot_t[...] = cot[...].T
    wn_t[...] = wn[...].T
    ws_t[...] = ws[...].T
    bias_sum[...] = jnp.sum(cot[...].astype(F32), axis=0, keepdims=True)
    wo_t = wo[...].T
    step = 256
    for r in range(0, rows, step):
        pre[r : r + step] = dot(x[r : r + step], ws[...]) + bias[...]
        half_act[r : r + step] = dot(cot[r : r + step], wo_t) * 0.5


def forward_kernel(
    place, cols, lo, x, hi, adj, x_t, cot_t, wn, pre, half_act, cot_sum, hid, dh, keep, send, bias,
    window, agg, left, sums
):
    rows, width = x.shape
    hidden = wn.shape[1]
    blocks, tile, _ = adj.shape
    slots = cols.shape[1]
    first, me, z = place[0], place[1], place[2]
    window[:rows] = lo[...]
    window[rows : 2 * rows] = x[...]
    window[2 * rows :] = hi[...]
    for b in range(blocks):
        parts = []
        for s in range(slots):
            at = pl.multiple_of((cols[b, s] - first) * tile, tile)
            parts.append(window[pl.ds(at, tile), :])
        agg[b * tile : (b + 1) * tile, :] = dot(adj[b], jnp.concatenate(parts, axis=0)).astype(BF16)
    left[:width] = x_t[...]
    left[width : 2 * width] = agg[...].T
    left[2 * width :] = jnp.ones((BIAS_ROWS, rows), BF16)
    chunk = 2 * LANES
    piece = width // QUARTERS
    core = lax.rem(me, 2)
    pair = me // 2
    sums[...] = jnp.zeros(sums.shape, F32)
    step = 512
    for c in range(hidden // chunk):
        at = slice(c * chunk, (c + 1) * chunk)
        for r in range(0, rows, step):
            sl = slice(r, r + step)
            v = dot(agg[sl], wn[:, at]) + pre[sl, at]
            sq = v * v
            t = jnp.tanh(v * (GELU_C + (GELU_C * GELU_A) * sq))
            h = 1.0 + t
            p = v * h
            hid[sl, at] = (0.5 * p).astype(BF16)
            slope = h + p * (GELU_C + (3.0 * GELU_C * GELU_A) * sq) * (1.0 - t)
            dh[sl, at] = (half_act[sl, at] * slope).astype(BF16)
        g = dot(left[...], dh[:, at])
        g_out = dot(cot_t[...], hid[:, at])
        for half in range(2):
            sums[2 * c + half : 2 * c + half + 1] = g[2 * width : 2 * width + 1, half * LANES : (half + 1) * LANES]
        base = jnp.bitwise_xor(c, pair) * QUARTERS
        for t, value in enumerate((g[:width], g[width : 2 * width], g_out)):
            mine = jnp.where(core == 0, value[:, :LANES], value[:, LANES:])
            other = jnp.where(core == 0, value[:, LANES:], value[:, :LANES]).astype(BF16)
            for k in range(QUARTERS):
                to = pl.multiple_of((base + jnp.bitwise_xor(k, z)) * (3 * piece) + t * piece, piece)
                keep[pl.ds(to, piece)] = mine[k * piece : (k + 1) * piece]
                send[pl.ds(to, piece)] = other[k * piece : (k + 1) * piece]
    top = hidden // LANES
    for i in range(width // LANES):
        sums[top + i : top + i + 1] = cot_sum[:, i * LANES : (i + 1) * LANES]
    high = sums[...].astype(BF16)
    low = (sums[...] - high.astype(F32)).astype(BF16)
    bias[...] = high.astype(F32) + low.astype(F32)
    end = send.shape[0] - 2 * BIAS_ROWS
    send[end : end + BIAS_ROWS] = high
    send[end + BIAS_ROWS :] = low


def spread_kernel(place, cols, adj, dh, wn_t, own, to_low, to_high, total, d_agg):
    rows, width = own.shape
    blocks, tile, _ = adj.shape
    slots = cols.shape[1]
    first = place[0]
    step = 256
    for r in range(0, rows, step):
        d_agg[r : r + step] = dot(dh[r : r + step], wn_t[...]).astype(BF16)
    total[...] = jnp.zeros(total.shape, F32)
    for b in range(blocks):
        spread = lax.dot_general(
            adj[b], d_agg[b * tile : (b + 1) * tile], (((0,), (0,)), ((), ())), preferred_element_type=F32
        )
        for s in range(slots):
            at = pl.multiple_of((cols[b, s] - first) * tile, tile)
            total[pl.ds(at, tile), :] += spread[s * tile : (s + 1) * tile]
    to_low[...] = total[:rows].astype(BF16)
    to_high[...] = total[2 * rows :].astype(BF16)
    own[...] = total[rows : 2 * rows]


def finish_kernel(hid, dh, wo, bias_out, ws_t, own, embed, near):
    rows = embed.shape[0]
    step = 256
    for r in range(0, rows, step):
        sl = slice(r, r + step)
        near[sl] = own[sl] + dot(dh[sl], ws_t[...])
        embed[sl] = (dot(hid[sl], wo[...]) + bias_out[...]).astype(BF16)


def place_grads(scale, half, place, src, outs, scratch):
    g_self, g_neigh, g_out = outs
    blocks, turned, flipped, sems = scratch
    width = g_self.shape[0]
    piece = width // QUARTERS
    me, z = place[1], place[2]
    copies = []
    for j in range(HALVES // 2):
        p = 2 * jnp.bitwise_xor(j, me // 2) + jnp.bitwise_xor(lax.rem(me, 2), half)
        at = pl.ds(pl.multiple_of(p * LANES, LANES), LANES)
        for k in range(QUARTERS):
            to = pl.ds(pl.multiple_of(jnp.bitwise_xor(k, z) * piece, piece), piece)
            blocks[0, j, to] = src[j, k, :piece].astype(F32) * scale
            blocks[1, j, to] = src[j, k, piece : 2 * piece].astype(F32) * scale
            turned[j, to] = src[j, k, 2 * piece :].astype(F32) * scale
        flipped[j] = turned[j].T
        copies.append(pltpu.make_async_copy(blocks.at[0, j], g_self.at[:, at], sems.at[j]))
        copies.append(pltpu.make_async_copy(blocks.at[1, j], g_neigh.at[:, at], sems.at[4 + j]))
        copies.append(pltpu.make_async_copy(flipped.at[j], g_out.at[at], sems.at[8 + j]))
        for copy in copies[-3:]:
            copy.start()
    return copies


def first_unpack_kernel(
    scale, place, src, own, from_low, from_high, bias,
    g_self, g_neigh, g_out, features, bias_hidden, bias_out, *scratch
):
    summed, done, *scratch = scratch
    summed[...] = (own[...] + from_low[...].astype(F32) + from_high[...].astype(F32)).astype(BF16)
    store = pltpu.make_async_copy(summed, features, done)
    store.start()
    copies = place_grads(scale, 0, place, src, (g_self, g_neigh, g_out), scratch)
    top, count = bias_hidden.shape[0], bias_out.shape[0]
    bias_hidden[...] = bias[:top] * scale
    bias_out[...] = bias[top : top + count] * scale
    for copy in copies:
        copy.wait()
    store.wait()


def second_unpack_kernel(scale, place, src, _0, _1, _2, g_self, g_neigh, g_out, *scratch):
    for copy in place_grads(scale, 1, place, src, (g_self, g_neigh, g_out), scratch):
        copy.wait()


def unpack_scratch(width):
    return [
        pltpu.VMEM((2, HALVES // 2, width, LANES), F32),
        pltpu.VMEM((HALVES // 2, width, LANES), F32),
        pltpu.VMEM((HALVES // 2, LANES, width), F32),
        pltpu.SemaphoreType.DMA((12,)),
    ]


def swap(value, axis, bit):
    return lax.ppermute(value, axis, [(i, i ^ bit) for i in range(lax.axis_size(axis))])


def swap_with_bias(value, bias, axis, bit):
    high = lax.reduce_precision(bias, 8, 7)
    low = lax.reduce_precision(bias - high, 8, 7)
    message = jnp.concatenate([value.reshape(-1, LANES), high.astype(BF16), low.astype(BF16)])
    got, theirs = received(swap(message, axis, bit), value.shape)
    return got, (high + low) + theirs


def received(message, shape):
    end = message.shape[0] - 2 * BIAS_ROWS
    bias = message[end : end + BIAS_ROWS].astype(F32) + message[end + BIAS_ROWS :].astype(F32)
    return message[:end].reshape(shape), bias


def reduce_first(keep, send, bias):
    shape = (HALVES // 2, QUARTERS, -1, LANES)
    got, theirs = received(swap(send, "row", 1), keep.shape)
    return (keep + got.astype(F32)).reshape(shape), bias + theirs


def reduce_among(parts, bias, axis, bits):
    high = lax.reduce_precision(bias, 8, 7)
    low = lax.reduce_precision(bias - high, 8, 7)
    extra = [high.astype(BF16), low.astype(BF16)]
    shape = parts[0].shape
    one, two, three = [
        received(swap(jnp.concatenate([v.astype(BF16).reshape(-1, LANES)] + extra), axis, bit), shape)
        for v, bit in zip(parts[1:], bits)
    ]
    total = (parts[0] + one[0].astype(F32)) + (two[0].astype(F32) + three[0].astype(F32))
    return total, ((high + low) + one[1]) + (two[1] + three[1])


def reduce_far(s, bias):
    bit = HALVES
    while bit < lax.axis_size("row"):
        s = s.astype(BF16)
        got, bias = swap_with_bias(s, bias, "row", bit)
        s = s.astype(F32) + got.astype(F32)
        bit *= 2
    return s.astype(BF16), bias


def gather_among(s, axis, bits):
    return jnp.stack([s] + [swap(s, axis, bit) for bit in bits])


def gather_near(s):
    a, b = s[:2], s[2:]
    return jnp.stack([a, swap(a, "row", 4)]), jnp.stack([b, swap(b, "row", 2)])


def gather_across(a, b):
    far_a, far_b = swap(a, "row", 2), swap(b, "row", 4)
    a = jnp.stack([a, far_a], axis=1).reshape((4,) + a.shape[1:])
    b = jnp.concatenate([b, far_b])
    return jnp.concatenate([a, b], axis=1)


def local(x, cols, tw, ws, wn, bias_hidden, wo, bias_out, cot):
    rows, width = x.shape
    hidden = ws.shape[1]
    blocks, tile, depth = tw.shape
    both = ("row", "col")
    count = lax.axis_size(both)
    tile_scale = 0.25 / math.sqrt(depth)
    grad_scale = 1.0 / math.sqrt(rows * count)
    forward = [(i, i + 1) for i in range(count - 1)]
    backward = [(j, i) for i, j in forward]
    place = jnp.stack(
        [
            lax.axis_index(both) * blocks - blocks,
            lax.rem(lax.axis_index("row"), HALVES),
            lax.axis_index("col"),
        ]
    ).astype(jnp.int32)
    sds = jax.ShapeDtypeStruct
    low = lax.ppermute(x, both, forward)
    high = lax.ppermute(x, both, backward)
    adj, x_t, cot_t, wn_t, ws_t, pre, half_act, cot_sum = pl.pallas_call(
        functools.partial(prepare_kernel, tile_scale),
        out_shape=(
            sds((blocks, tile, depth), BF16),
            sds((width, rows), BF16),
            sds((width, rows), BF16),
            sds((hidden, width), BF16),
            sds((hidden, width), BF16),
            sds((rows, hidden), F32),
            sds((rows, hidden), F32),
            sds((1, width), F32),
        ),
        in_specs=[vmem()] * 7,
        out_specs=[vmem()] * 8,
        compiler_params=params(22),
        cost_estimate=pl.CostEstimate(flops=4 * rows * width * hidden, bytes_accessed=9 << 20, transcendentals=0),
        name="prepare",
    )(tw, x, cot, ws, wn, wo, bias_hidden.reshape(1, -1))
    size = HALVES // 2 * 3 * width
    hid, dh, keep, send, bias = pl.pallas_call(
        forward_kernel,
        out_shape=(
            sds((rows, hidden), BF16),
            sds((rows, hidden), BF16),
            sds((size, LANES), F32),
            sds((size + 2 * BIAS_ROWS, LANES), BF16),
            sds((BIAS_ROWS, LANES), F32),
        ),
        in_specs=[smem(), smem()] + [vmem()] * 10,
        out_specs=[vmem()] * 5,
        scratch_shapes=[
            pltpu.VMEM((3 * rows, width), BF16),
            pltpu.VMEM((rows, width), BF16),
            pltpu.VMEM((2 * width + BIAS_ROWS, rows), BF16),
            pltpu.VMEM((BIAS_ROWS, LANES), F32),
        ],
        compiler_params=params(30),
        cost_estimate=pl.CostEstimate(
            flops=2 * rows * width * (4 * hidden + depth), bytes_accessed=14 << 20, transcendentals=rows * hidden
        ),
        name="forward",
    )(place, cols, low, x, high, adj, x_t, cot_t, wn, pre, half_act, cot_sum)
    acc, bias = reduce_first(keep, send, bias)
    acc, dh, hid = lax.optimization_barrier((acc, dh, hid))
    own, to_low, to_high = pl.pallas_call(
        spread_kernel,
        out_shape=(sds((rows, width), F32), sds((rows, width), BF16), sds((rows, width), BF16)),
        in_specs=[smem(), smem()] + [vmem()] * 3,
        out_specs=[vmem()] * 3,
        scratch_shapes=[pltpu.VMEM((3 * rows, width), F32), pltpu.VMEM((rows, width), BF16)],
        compiler_params=params(16),
        cost_estimate=pl.CostEstimate(
            flops=2 * rows * width * (hidden + depth), bytes_accessed=6 << 20, transcendentals=0
        ),
        name="spread",
    )(place, cols, adj, dh, wn_t)
    acc, bias = reduce_among([acc[i] for i in range(4)], bias, "row", (2, 4, 6))
    end = rows // 2
    acc, hid, dh, own = lax.optimization_barrier((acc, hid, dh, own))
    embed, own = pl.pallas_call(
        finish_kernel,
        out_shape=(sds((rows, width), BF16), sds((rows, width), F32)),
        in_specs=[vmem()] * 6,
        out_specs=[vmem()] * 2,
        compiler_params=params(12),
        cost_estimate=pl.CostEstimate(flops=4 * rows * width * hidden, bytes_accessed=8 << 20, transcendentals=0),
        name="finish",
    )(hid, dh, wo, bias_out.reshape(1, -1), ws_t, own)
    part, bias = reduce_among([acc[i] for i in range(4)], bias, "col", (1, 2, 3))
    second = lax.ppermute(to_high[0:end], both, forward)
    part, second, to_low, to_high, embed, own = lax.optimization_barrier((part, second, to_low, to_high, embed, own))
    part, bias = reduce_far(part, bias)
    from_high = lax.ppermute(to_low, both, backward)
    last = lax.ppermute(to_high[end:], both, forward)
    part = gather_among(part, "col", (1, 2, 3))
    a, b = gather_near(part)
    a, b, last = lax.optimization_barrier((a, b, last))
    mine = gather_across(a, b)
    mine, from_high = lax.optimization_barrier((mine, from_high))
    from_low = jnp.concatenate([second, last])
    other = swap(mine, "row", 1)
    anywhere = pl.BlockSpec(memory_space=pl.ANY)
    grads = (sds((width, hidden), F32), sds((width, hidden), F32), sds((hidden, width), F32))
    *grads_half, grad_features, bias_h, bias_o = pl.pallas_call(
        functools.partial(first_unpack_kernel, grad_scale),
        out_shape=grads
        + (sds((rows, width), BF16), sds((hidden // LANES, LANES), F32), sds((width // LANES, LANES), F32)),
        in_specs=[smem()] + [vmem()] * 5,
        out_specs=[anywhere] * 4 + [vmem()] * 2,
        scratch_shapes=[pltpu.VMEM((rows, width), BF16), pltpu.SemaphoreType.DMA] + unpack_scratch(width),
        compiler_params=params(10),
        cost_estimate=pl.CostEstimate(flops=4 * width * hidden, bytes_accessed=12 * width * hidden, transcendentals=0),
        name="first_unpack",
    )(place, mine, own, from_low, from_high, bias)
    g_self, g_neigh, g_out = pl.pallas_call(
        functools.partial(second_unpack_kernel, grad_scale),
        out_shape=grads,
        in_specs=[smem(), vmem()] + [anywhere] * 3,
        out_specs=[anywhere] * 3,
        input_output_aliases={2: 0, 3: 1, 4: 2},
        scratch_shapes=unpack_scratch(width),
        compiler_params=params(8),
        cost_estimate=pl.CostEstimate(flops=2 * width * hidden, bytes_accessed=9 * width * hidden, transcendentals=0),
        name="second_unpack",
    )(place, other, *grads_half)
    return embed, grad_features, g_self, g_neigh, bias_h.reshape(-1), g_out, bias_o.reshape(-1)


def solution(mesh):
    share = P(("row", "col"), None)
    in_specs = (share, share, P(("row", "col"), None, None), P(), P(), P(), P(), P(), share)
    out_specs = (share, share, P(), P(), P(), P(), P())
    return jax.shard_map(local, mesh=mesh, in_specs=in_specs, out_specs=out_specs, check_vma=False)
```
